32 devices in a mesh: outer: 8 (over z, y), inner: 4 (over x, core).
Axes of the slice: x: 2, y: 2, z: 4, core: 2. Of those that a mesh axis runs over, the one named last changes fastest.
Arguments:
- stem_real: float32 [8, 4, 256, 512], P('outer', 'inner'), may hold values from -6 to 6
- stem_imag: float32 [8, 4, 256, 512], P('outer', 'inner'), may hold values from -6 to 6
- branch_real: float32 [4, 512, 512], replicated, may hold values from -0.1875 to 0.1875
- branch_imag: float32 [4, 512, 512], replicated, may hold values from -0.1875 to 0.1875
- orders: int32 [4, 512], replicated, may hold values from 0 to 511, each once within a row
Outputs:
- out_real: float32 [8, 4, 256, 512], P('outer', 'inner')
- out_imag: float32 [8, 4, 256, 512], P('outer', 'inner')
The draws below stay inside these ranges and needn't reach their ends.
Inputs may be any that keep to these rules, and one draw needn't show every extreme that they name: Each row of orders holds every index of 0 to 511 once.
All inputs are finite; a program needn't handle non-finite values.
Results may differ from the reference program's by a relative error of at most 0.0001.
Values sent between devices are 32-bit elements; how exact they have to be, the bound alone decides.
A program may use at most 64 MiB of HBM per device.

```python
import jax
import jax.numpy as jnp
from jax import lax

K = 512
ROWS = 256
PRODUCTS = 4
N_OUTER = 8
N_INNER = 4


def shard_levels(own_key, shape, pieces, least, high):
    loudness = 1.0
    for position, shards_of in pieces:
        draws = jax.random.uniform(jax.random.fold_in(jax.random.fold_in(own_key, 6), position), (shards_of,), jnp.float32, least / len(pieces), high / len(pieces))
        loudness = loudness * jnp.repeat(jnp.exp(draws), shape[position] // shards_of).reshape((-1,) + (1,) * (len(shape) - 1 - position))
    return loudness


def scatter_about(own_key, extent, spread, bound, cuts=(), dtype=jnp.bfloat16):
    values = spread * jax.random.normal(own_key, extent, jnp.float32)
    if cuts:
        values = values * shard_levels(own_key, extent, cuts, -0.22, 0.18)
    return jnp.clip(values, -bound, bound).astype(dtype)


def setup_inputs(seed: int = 0) -> dict:
    arg_keys = jax.random.split(jax.random.key(seed), 6)
    return {
        "stem_real": scatter_about(arg_keys[0], (N_OUTER, N_INNER, ROWS, K), 1.0, 6.0, ((0, 8), (1, 4)), jnp.float32),
        "stem_imag": scatter_about(arg_keys[1], (N_OUTER, N_INNER, ROWS, K), 1.0, 6.0, ((0, 8), (1, 4)), jnp.float32),
        "branch_real": scatter_about(arg_keys[2], (PRODUCTS, K, K), (2 * K) ** -0.5, 0.1875, (), jnp.float32),
        "branch_imag": scatter_about(arg_keys[3], (PRODUCTS, K, K), (2 * K) ** -0.5, 0.1875, (), jnp.float32),
        "orders": jax.vmap(lambda own: jax.random.permutation(own, K))(jax.random.split(arg_keys[4], PRODUCTS)).reshape((PRODUCTS, K)).astype(jnp.int32),
    }


def multiply(plane_real, plane_imag, branch_real, branch_imag, order):
    shape = plane_real.shape
    width = shape[-1]
    left_real = plane_real[..., order].reshape(-1, width)
    left_imag = plane_imag[..., order].reshape(-1, width)
    first = jnp.dot(left_real, branch_real, precision=lax.Precision.HIGHEST, preferred_element_type=jnp.float32)
    second = jnp.dot(left_imag, branch_imag, precision=lax.Precision.HIGHEST, preferred_element_type=jnp.float32)
    third = jnp.dot(left_real + left_imag, branch_real + branch_imag, precision=lax.Precision.HIGHEST, preferred_element_type=jnp.float32)
    return (first - second).reshape(shape), (third - first - second).reshape(shape)


def swap_group(plane, groups, axis_pos):
    outer_n, inner_n, rows_n, width = plane.shape
    viewed = plane.reshape(outer_n, inner_n, rows_n, groups, width // groups)
    viewed = jnp.swapaxes(viewed, axis_pos, 3)
    return viewed.reshape(outer_n, inner_n, rows_n, width)


def reference(stem_real, stem_imag, branch_real, branch_imag, orders):
    plane_real, plane_imag = multiply(stem_real, stem_imag, branch_real[0], branch_imag[0], orders[0])
    plane_real = swap_group(plane_real, N_INNER, 1)
    plane_imag = swap_group(plane_imag, N_INNER, 1)
    plane_real, plane_imag = multiply(plane_real, plane_imag, branch_real[1], branch_imag[1], orders[1])
    plane_real = swap_group(plane_real, N_OUTER, 0)
    plane_imag = swap_group(plane_imag, N_OUTER, 0)
    plane_real, plane_imag = multiply(plane_real, plane_imag, branch_real[2], branch_imag[2], orders[2])
    plane_real = swap_group(plane_real, N_INNER, 1)
    plane_imag = swap_group(plane_imag, N_INNER, 1)
    plane_real, plane_imag = multiply(plane_real, plane_imag, branch_real[3], branch_imag[3], orders[3])
    return plane_real, plane_imag
```

```python
import functools

import jax
import jax.numpy as jnp
from jax import lax
from jax.experimental import pallas as pl
from jax.experimental.pallas import tpu as pltpu
from jax.sharding import PartitionSpec as P

MESH = pl.DeviceIdType.MESH
LANES = 128
CHUNKS = 4
F32 = jnp.float32
BF16 = jnp.bfloat16


def prepare(branch_real, branch_imag, order):
    width = branch_real.shape[0]
    places = lax.broadcasted_iota(jnp.int32, (width, width), 0)
    selector = (places == order[None, :]).astype(F32)
    dot = functools.partial(jnp.dot, precision=lax.Precision.HIGHEST, preferred_element_type=F32)
    moved_real = dot(selector, branch_real)
    moved_imag = dot(selector, branch_imag)
    return (moved_real, moved_imag, moved_real + moved_imag)


def product(plane_real, plane_imag, prepared):
    moved_real, moved_imag, moved_sum = prepared
    width = moved_real.shape[0]
    count = plane_real.size // width
    dot = functools.partial(jnp.dot, precision=lax.Precision.HIGHEST, preferred_element_type=F32)
    left_real = plane_real.reshape(count, width)
    left_imag = plane_imag.reshape(count, width)
    first = dot(left_real, moved_real)
    second = dot(left_imag, moved_imag)
    third = dot(left_real + left_imag, moved_sum)
    return (
        (first - second).reshape(1, 1, count, width),
        (third - first - second).reshape(1, 1, count, width),
    )


def general(stem_real, stem_imag, branch_real, branch_imag, orders):
    planes = (stem_real, stem_imag)
    swaps = ("inner", "outer", "inner")
    for step in range(branch_real.shape[0]):
        if step:
            planes = [
                lax.all_to_all(x, swaps[step - 1], split_axis=3, concat_axis=3, tiled=True)
                for x in planes
            ]
        planes = product(*planes, prepare(branch_real[step], branch_imag[step], orders[step]))
    return tuple(planes)


def split(x):
    high = x.astype(BF16)
    low = (x - high.astype(F32)).astype(BF16)
    return high, low


def lay_columns(first, second, groups):
    width = first.shape[1]
    share = width // groups
    if share % LANES == 0:
        parts = []
        for g in range(groups):
            parts.append(first[:, g * share : (g + 1) * share])
            parts.append(second[:, g * share : (g + 1) * share])
        return jnp.concatenate(parts, axis=1)
    lower = lax.broadcasted_iota(jnp.int32, (first.shape[0], LANES), 1) < share
    parts = []
    for t in range(width // LANES):
        a = first[:, t * LANES : (t + 1) * LANES]
        b = second[:, t * LANES : (t + 1) * LANES]
        parts.append(jnp.where(lower, a, pltpu.roll(b, share, 1)))
        parts.append(jnp.where(lower, pltpu.roll(a, share, 1), b))
    return jnp.concatenate(parts, axis=1)


def build(order_ref, real_ref, imag_ref, high_ref, low_ref, step, groups_in, groups_out):
    width = real_ref.shape[1]
    share = width // groups_in
    order = order_ref[step : step + 1, :]
    block = min(256, width)
    real_terms = split(real_ref[step])
    imag_terms = split(imag_ref[step])
    for start in range(0, width, block):
        places = lax.broadcasted_iota(jnp.int32, (block, width), 0) + start
        selector = jnp.where(places == order, 1.0, 0.0).astype(BF16)
        for term, out_ref in enumerate((high_ref, low_ref)):
            moved_real = jnp.dot(selector, real_terms[term], preferred_element_type=F32)
            moved_imag = jnp.dot(selector, imag_terms[term], preferred_element_type=F32)
            top = lay_columns(moved_real, moved_imag, groups_out).astype(BF16)
            bottom = lay_columns(-moved_imag, moved_real, groups_out).astype(BF16)
            run = min(share, block)
            for at in range(start, start + block, run):
                group, place = divmod(at, share)
                row = group * 2 * share + place
                part = slice(at - start, at - start + run)
                out_ref[row : row + run, :] = top[part]
                out_ref[row + share : row + share + run, :] = bottom[part]


def kernel(
    axes,
    sizes,
    order_ref,
    stem_real,
    stem_imag,
    branch_real,
    branch_imag,
    out_real,
    out_imag,
    stem,
    real,
    imag,
    highs,
    lows,
    sent0,
    sent1,
    sent2,
    got0,
    got1,
    got2,
    load_sem,
    branch_sem,
    send0,
    send1,
    send2,
    recv0,
    recv1,
    recv2,
):
    products = branch_real.shape[0]
    sent, got = (sent0, sent1, sent2), (got0, got1, got2)
    send_sems, recv_sems = (send0, send1, send2), (recv0, recv1, recv2)
    rows, width = stem_real.shape
    part = rows // CHUNKS
    me = [lax.axis_index(a) for a in axes]

    loads = [
        pltpu.make_async_copy(stem_real, stem.at[0], load_sem.at[0]),
        pltpu.make_async_copy(stem_imag, stem.at[1], load_sem.at[1]),
    ]
    fetches = [
        (
            pltpu.make_async_copy(branch_real.at[p], real.at[p], branch_sem.at[p, 0]),
            pltpu.make_async_copy(branch_imag.at[p], imag.at[p], branch_sem.at[p, 1]),
        )
        for p in range(products)
    ]
    for copy in fetches[0]:
        copy.start()
    for copy in loads:
        copy.start()
    for pair in fetches[1:]:
        for copy in pair:
            copy.start()

    barrier = pltpu.get_barrier_semaphore()
    partners = 0
    for axis in sorted(set(axes)):
        size = sizes[axis]
        mine = lax.axis_index(axis)
        for s in range(1, size):
            pl.semaphore_signal(
                barrier,
                inc=1,
                device_id={axis: lax.rem(mine + s, size)},
                device_id_type=MESH,
            )
            partners += 1

    groups = [1] + [sizes[a] for a in axes] + [1]

    def prep(p):
        for copy in fetches[p]:
            copy.wait()
        build(order_ref, real, imag, highs.at[p], lows.at[p], p, groups[p], groups[p + 1])

    def swap_copy(p, c, s, arriving):
        size = sizes[axes[p]]
        there = lax.rem(me[p] + s, size)
        slot = lax.rem(me[p] + size - s, size) if arriving else me[p]
        return pltpu.make_async_remote_copy(
            src_ref=sent[p].at[there, c],
            dst_ref=got[p].at[slot, c],
            send_sem=send_sems[p].at[c, s - 1],
            recv_sem=recv_sems[p].at[c, s - 1],
            device_id={axes[p]: there},
            device_id_type=MESH,
        )

    def multiply(p, c):
        if p == 0:
            at = pl.ds(pl.multiple_of(c * part, part), part)
            x = jnp.concatenate([stem[0, at, :], stem[1, at, :]], axis=1)
        else:
            for s in range(1, groups[p]):
                swap_copy(p - 1, c, s, True).wait_recv()
            x = jnp.concatenate([got[p - 1][g, c] for g in range(groups[p])], axis=1)
        high, low = split(x)
        both = jnp.concatenate([high, low], axis=0)
        lanes = 2 * width // groups[p + 1]
        block = min(256, 2 * width)
        for start in range(0, 2 * width, block):
            cols = slice(start, start + block)
            y = jnp.dot(both, highs[p, :, cols], preferred_element_type=F32)
            y = y[:part] + y[part:]
            y = y + jnp.dot(high, lows[p, :, cols], preferred_element_type=F32)
            if p == products - 1:
                at = pl.ds(pl.multiple_of(c * part, part), part)
                if start < width:
                    out_real[at, start : start + block] = y
                else:
                    out_imag[at, start - width : start - width + block] = y
            else:
                run = min(block, lanes)
                for k in range(0, block, run):
                    group, place = divmod(start + k, lanes)
                    sent[p][group, c, :, place : place + run] = y[:, k : k + run]
        if p < products - 1:
            if p == 0:
                pass
            for s in range(1, groups[p + 1]):
                swap_copy(p, c, s, False).start()
            got[p][me[p], c] = sent[p][me[p], c]

    def stage(p):
        @pl.loop(0, CHUNKS)
        def _(c):
            multiply(p, c)

    prep(0)
    for copy in loads:
        copy.wait()
    pl.semaphore_wait(barrier, partners)
    stage(0)
    prep(1)
    stage(1)
    for p in range(2, products):
        prep(p)
    stage(2)
    stage(3)

    for p in range(len(axes)):

        @pl.loop(0, CHUNKS)
        def _(c):
            for s in range(1, sizes[axes[p]]):
                swap_copy(p, c, s, False).wait_send()


def fused(sizes, stem_real, stem_imag, branch_real, branch_imag, orders):
    rows, width = stem_real.shape[-2:]
    products = branch_real.shape[0]
    axes = ("inner", "outer", "inner")
    part = rows // CHUNKS

    def buffers():
        return [
            pltpu.VMEM((sizes[a], CHUNKS, part, 2 * width // sizes[a]), F32) for a in axes
        ]

    def semaphores():
        return [pltpu.SemaphoreType.DMA((CHUNKS, sizes[a] - 1)) for a in axes]

    plane = jax.ShapeDtypeStruct((rows, width), F32)
    flops = products * 3 * 2 * rows * (2 * width) ** 2 + products * 8 * width**3
    out_real, out_imag = pl.pallas_call(
        functools.partial(kernel, axes, sizes),
        out_shape=(plane, plane),
        in_specs=[pl.BlockSpec(memory_space=pltpu.VMEM)]
        + [pl.BlockSpec(memory_space=pl.ANY)] * 4,
        out_specs=(pl.BlockSpec(memory_space=pltpu.VMEM),) * 2,
        scratch_shapes=[
            pltpu.VMEM((2, rows, width), F32),
            pltpu.VMEM((products, width, width), F32),
            pltpu.VMEM((products, width, width), F32),
            pltpu.VMEM((products, 2 * width, 2 * width), BF16),
            pltpu.VMEM((products, 2 * width, 2 * width), BF16),
        ]
        + buffers()
        + buffers()
        + [pltpu.SemaphoreType.DMA((2,)), pltpu.SemaphoreType.DMA((products, 2))]
        + semaphores()
        + semaphores(),
        compiler_params=pltpu.CompilerParams(
            collective_id=0, has_side_effects=True, vmem_limit_bytes=56 * 2**20
        ),
        cost_estimate=pl.CostEstimate(
            flops=flops, bytes_accessed=4 * (branch_real.size * 2 + rows * width * 4), transcendentals=0
        ),
    )(
        orders,
        stem_real.reshape(rows, width),
        stem_imag.reshape(rows, width),
        branch_real,
        branch_imag,
    )
    return out_real.reshape(stem_real.shape), out_imag.reshape(stem_imag.shape)


def fits(sizes, rows, width):
    shares = [width // size for size in sizes.values()]
    return (
        all(share % LANES == 0 or 2 * share == LANES for share in shares)
        and rows % (CHUNKS * 16) == 0
        and width % 256 == 0
    )


def solution(mesh):
    sizes = {axis: mesh.shape[axis] for axis in ("outer", "inner")}

    def on_device(stem_real, stem_imag, branch_real, branch_imag, orders):
        arrays = (stem_real, stem_imag, branch_real, branch_imag, orders)
        if fits(sizes, *stem_real.shape[-2:]):
            return fused(sizes, *arrays)
        return general(*arrays)

    planes = P("outer", "inner", None, None)
    return jax.shard_map(
        on_device,
        mesh=mesh,
        in_specs=(planes, planes, P(), P(), P()),
        out_specs=(planes, planes),
        check_vma=False,
    )
```

```python
import functools

import jax
import jax.numpy as jnp
from jax import lax
from jax.experimental import pallas as pl
from jax.experimental.pallas import tpu as pltpu
from jax.sharding import PartitionSpec as P

MESH = pl.DeviceIdType.MESH
LANES = 128
SHARES = (1, 2, 2, 2, 1)
F32 = jnp.float32
BF16 = jnp.bfloat16


def prepare(branch_real, branch_imag, order):
    width = branch_real.shape[0]
    places = lax.broadcasted_iota(jnp.int32, (width, width), 0)
    selector = (places == order[None, :]).astype(F32)
    dot = functools.partial(jnp.dot, precision=lax.Precision.HIGHEST, preferred_element_type=F32)
    moved_real = dot(selector, branch_real)
    moved_imag = dot(selector, branch_imag)
    return (moved_real, moved_imag, moved_real + moved_imag)


def product(plane_real, plane_imag, prepared):
    moved_real, moved_imag, moved_sum = prepared
    width = moved_real.shape[0]
    count = plane_real.size // width
    dot = functools.partial(jnp.dot, precision=lax.Precision.HIGHEST, preferred_element_type=F32)
    left_real = plane_real.reshape(count, width)
    left_imag = plane_imag.reshape(count, width)
    first = dot(left_real, moved_real)
    second = dot(left_imag, moved_imag)
    third = dot(left_real + left_imag, moved_sum)
    return (
        (first - second).reshape(1, 1, count, width),
        (third - first - second).reshape(1, 1, count, width),
    )


def general(stem_real, stem_imag, branch_real, branch_imag, orders):
    planes = (stem_real, stem_imag)
    swaps = ("inner", "outer", "inner")
    for step in range(branch_real.shape[0]):
        if step:
            planes = [
                lax.all_to_all(x, swaps[step - 1], split_axis=3, concat_axis=3, tiled=True)
                for x in planes
            ]
        planes = product(*planes, prepare(branch_real[step], branch_imag[step], orders[step]))
    return tuple(planes)


def split(x):
    high = x.astype(BF16)
    low = (x - high.astype(F32)).astype(BF16)
    return high, low


def lay_columns(first, second, groups):
    width = first.shape[1]
    share = width // groups
    parts = []
    if share % LANES == 0:
        for g in range(groups):
            parts.append(first[:, g * share : (g + 1) * share])
            parts.append(second[:, g * share : (g + 1) * share])
        return jnp.concatenate(parts, axis=1)
    lower = lax.broadcasted_iota(jnp.int32, (first.shape[0], LANES), 1) < share
    for t in range(width // LANES):
        a = first[:, t * LANES : (t + 1) * LANES]
        b = second[:, t * LANES : (t + 1) * LANES]
        parts.append(jnp.where(lower, a, pltpu.roll(b, share, 1)))
        parts.append(jnp.where(lower, pltpu.roll(a, share, 1), b))
    return jnp.concatenate(parts, axis=1)


def part_planes(blocks):
    lanes = blocks[0].shape[1]
    share = lanes // 2
    if share % LANES == 0:
        return (
            jnp.concatenate([x[:, :share] for x in blocks], axis=1),
            jnp.concatenate([x[:, share:] for x in blocks], axis=1),
        )
    lower = lax.broadcasted_iota(jnp.int32, blocks[0].shape, 1) < share
    real, imag = [], []
    for a, b in zip(blocks[::2], blocks[1::2]):
        real.append(jnp.where(lower, a, pltpu.roll(b, share, 1)))
        imag.append(jnp.where(lower, pltpu.roll(a, share, 1), b))
    return jnp.concatenate(real, axis=1), jnp.concatenate(imag, axis=1)


def build(order_ref, real_ref, imag_ref, high_ref, low_ref, step, groups_out):
    width = real_ref.shape[1]
    order = order_ref[step : step + 1, :]
    block = min(256, width)
    real_terms = split(real_ref[step])
    imag_terms = split(imag_ref[step])
    for start in range(0, width, block):
        places = lax.broadcasted_iota(jnp.int32, (block, width), 0) + start
        selector = jnp.where(places == order, 1.0, 0.0).astype(BF16)
        for term, out_ref in enumerate((high_ref, low_ref)):
            moved_real = jnp.dot(selector, real_terms[term], preferred_element_type=F32)
            moved_imag = jnp.dot(selector, imag_terms[term], preferred_element_type=F32)
            laid = lay_columns(moved_real, moved_imag, groups_out)
            out_ref[start : start + block, :] = laid.astype(BF16)


def kernel(
    axes,
    sizes,
    chunks,
    orders,
    stem_real,
    stem_imag,
    branch_real,
    branch_imag,
    out_real,
    out_imag,
    order_ref,
    stem,
    done,
    real,
    imag,
    highs,
    lows,
    sent0,
    sent1,
    sent2,
    got0,
    got1,
    got2,
    load_sem,
    branch_sem,
    out_sem,
    send0,
    send1,
    send2,
    recv0,
    recv1,
    recv2,
):
    products = branch_real.shape[0]
    sent, got = (sent0, sent1, sent2), (got0, got1, got2)
    send_sems, recv_sems = (send0, send1, send2), (recv0, recv1, recv2)
    rows, width = stem_real.shape
    me = [lax.axis_index(a) for a in axes]
    last = products - 1
    places = []
    for c, size in enumerate(chunks):
        at = sum(chunks[:c])
        places.append(slice(at, at + size))

    loads = [
        pltpu.make_async_copy(orders, order_ref, load_sem.at[2]),
        pltpu.make_async_copy(stem_real, stem.at[0], load_sem.at[0]),
        pltpu.make_async_copy(stem_imag, stem.at[1], load_sem.at[1]),
    ]
    fetches = [
        (
            pltpu.make_async_copy(branch_real.at[p], real.at[p], branch_sem.at[p, 0]),
            pltpu.make_async_copy(branch_imag.at[p], imag.at[p], branch_sem.at[p, 1]),
        )
        for p in range(products)
    ]
    for copy in (loads[0], *fetches[0], *loads[1:]):
        copy.start()
    for pair in fetches[1:]:
        for copy in pair:
            copy.start()

    barrier = pltpu.get_barrier_semaphore()
    partners = 0
    for axis in sorted(set(axes)):
        size = sizes[axis]
        mine = lax.axis_index(axis)
        for s in range(1, size):
            pl.semaphore_signal(
                barrier,
                inc=1,
                device_id={axis: lax.rem(mine + s, size)},
                device_id_type=MESH,
            )
            partners += 1

    groups = [1] + [sizes[a] for a in axes] + [1]

    def prep(p):
        for copy in fetches[p]:
            copy.wait()
        build(order_ref, real, imag, highs.at[p], lows.at[p], p, groups[p + 1])

    def swap_copy(p, c, s, arriving):
        size = sizes[axes[p]]
        there = lax.rem(me[p] + s, size)
        slot = lax.rem(me[p] + size - s, size) if arriving else me[p]
        return pltpu.make_async_remote_copy(
            src_ref=sent[p].at[there, places[c]],
            dst_ref=got[p].at[slot, places[c]],
            send_sem=send_sems[p].at[c, s - 1],
            recv_sem=recv_sems[p].at[c, s - 1],
            device_id={axes[p]: there},
            device_id_type=MESH,
        )

    def out_copies(c):
        return (
            pltpu.make_async_copy(
                done.at[0, places[c]], out_real.at[places[c]], out_sem.at[c, 0]
            ),
            pltpu.make_async_copy(
                done.at[1, places[c]], out_imag.at[places[c]], out_sem.at[c, 1]
            ),
        )

    def multiply(p, c):
        size, at = chunks[c], places[c]
        if p == 0:
            xr, xi = stem[0, at, :], stem[1, at, :]
        else:
            for s in range(1, groups[p]):
                swap_copy(p - 1, c, s, True).wait_recv()
            xr, xi = part_planes([got[p - 1][g, at] for g in range(groups[p])])
        high, low = split(jnp.concatenate([xr, xi], axis=0))
        both = jnp.concatenate([high, low], axis=0)

        def columns(start, stop):
            cols = slice(start, stop)
            y = jnp.dot(both, highs[p, :, cols], preferred_element_type=F32)
            y = y[: 2 * size] + y[2 * size :]
            y = y + jnp.dot(high, lows[p, :, cols], preferred_element_type=F32)
            return y[:size], y[size:]

        share = width // groups[p + 1]
        if share % LANES == 0:
            run = min(share, LANES if p < last else 256)
            for group in range(groups[p + 1]):
                for place in range(0, share, run):
                    base = group * 2 * share + place
                    if run == share:
                        yr, yi = columns(base, base + 2 * share)
                        rr, ri = yr[:, :share], yr[:, share:]
                        ir, ii = yi[:, :share], yi[:, share:]
                    else:
                        rr, ir = columns(base, base + run)
                        ri, ii = columns(base + share, base + share + run)
                    if p == last:
                        done[0, at, place : place + run] = rr - ii
                        done[1, at, place : place + run] = ri + ir
                    else:
                        sent[p][group, at, place : place + run] = rr - ii
                        sent[p][group, at, share + place : share + place + run] = ri + ir
        else:
            lower = lax.broadcasted_iota(jnp.int32, (size, LANES), 1) < share
            for group in range(0, groups[p + 1], 2):
                yr, yi = columns(group * LANES, (group + 2) * LANES)
                for k in range(2):
                    a = yr[:, k * LANES : (k + 1) * LANES]
                    b = pltpu.roll(yi[:, k * LANES : (k + 1) * LANES], share, 1)
                    sent[p][group + k, at, :] = a + jnp.where(lower, -b, b)
        if p == last:
            for copy in out_copies(c):
                copy.start()
        else:
            if p == 0 and c == 0:
                pl.semaphore_wait(barrier, partners)
            for s in range(1, groups[p + 1]):
                swap_copy(p, c, s, False).start()
            got[p][me[p], at] = sent[p][me[p], at]

    count = len(chunks)
    loads[0].wait()
    prep(0)
    for copy in loads[1:]:
        copy.wait()
    for c in range(min(2, count)):
        multiply(0, c)
    prep(1)
    for c in range(count):
        multiply(1, c)
        if c + 2 < count:
            multiply(0, c + 2)
        if c == 0:
            prep(2)
        if c == 1:
            prep(3)
    multiply(2, 0)
    for c in range(1, count):
        multiply(2, c)
        multiply(3, c - 1)
    multiply(3, count - 1)

    for c in range(count):
        for p in range(len(axes)):
            for s in range(1, sizes[axes[p]]):
                swap_copy(p, c, s, False).wait_send()
        for copy in out_copies(c):
            copy.wait()


def deliver(real, imag, out_real, out_imag):
    out_real[...] = real[...]
    out_imag[...] = imag[...]


def fused(sizes, stem_real, stem_imag, branch_real, branch_imag, orders):
    rows, width = stem_real.shape[-2:]
    products = branch_real.shape[0]
    axes = ("inner", "outer", "inner")
    chunks = [rows * n // sum(SHARES) for n in SHARES]
    anywhere = pl.BlockSpec(memory_space=pltpu.HBM)

    buffers = [pltpu.VMEM((sizes[a], rows, 2 * width // sizes[a]), F32) for a in axes]
    semaphores = [pltpu.SemaphoreType.DMA((len(chunks), sizes[a] - 1)) for a in axes]
    plane = jax.ShapeDtypeStruct((rows, width), F32)
    flops = products * 3 * 2 * rows * (2 * width) ** 2 + products * 8 * width**3
    planes = pl.pallas_call(
        functools.partial(kernel, axes, sizes, chunks),
        out_shape=(plane, plane),
        in_specs=[anywhere] * 5,
        out_specs=(anywhere, anywhere),
        scratch_shapes=[
            pltpu.VMEM(orders.shape, orders.dtype),
            pltpu.VMEM((2, rows, width), F32),
            pltpu.VMEM((2, rows, width), F32),
            pltpu.VMEM((products, width, width), F32),
            pltpu.VMEM((products, width, width), F32),
            pltpu.VMEM((products, width, 2 * width), BF16),
            pltpu.VMEM((products, width, 2 * width), BF16),
        ]
        + buffers * 2
        + [
            pltpu.SemaphoreType.DMA((3,)),
            pltpu.SemaphoreType.DMA((products, 2)),
            pltpu.SemaphoreType.DMA((len(chunks), 2)),
        ]
        + semaphores * 2,
        compiler_params=pltpu.CompilerParams(
            collective_id=0, has_side_effects=True, vmem_limit_bytes=56 * 2**20
        ),
        cost_estimate=pl.CostEstimate(
            flops=flops,
            bytes_accessed=4 * (branch_real.size * 2 + rows * width * 4),
            transcendentals=0,
        ),
    )(
        orders,
        stem_real.reshape(rows, width),
        stem_imag.reshape(rows, width),
        branch_real,
        branch_imag,
    )
    whole = pl.BlockSpec(memory_space=pltpu.VMEM)
    planes = pl.pallas_call(
        deliver,
        out_shape=(plane, plane),
        in_specs=[whole, whole],
        out_specs=(whole, whole),
    )(*planes)
    return tuple(x.reshape(stem_real.shape) for x in planes)


def fits(sizes, rows, width):
    shares = [width // size for size in sizes.values()]
    return (
        all(share % LANES == 0 or 2 * share == LANES for share in shares)
        and rows % (sum(SHARES) * 16) == 0
        and width % 256 == 0
    )


def solution(mesh):
    sizes = {axis: mesh.shape[axis] for axis in ("outer", "inner")}

    def on_device(stem_real, stem_imag, branch_real, branch_imag, orders):
        arrays = (stem_real, stem_imag, branch_real, branch_imag, orders)
        if fits(sizes, *stem_real.shape[-2:]):
            return fused(sizes, *arrays)
        return general(*arrays)

    planes = P("outer", "inner", None, None)
    return jax.shard_map(
        on_device,
        mesh=mesh,
        in_specs=(planes, planes, P(), P(), P()),
        out_specs=(planes, planes),
        check_vma=False,
    )
```
